512 devices in a mesh: dp: 4 (over x), expert: 128 (over z, y, core).
Axes of the slice: x: 4, y: 4, z: 16, core: 2. Of those that a mesh axis runs over, the one named last changes fastest.
Arguments:
- tokens: bfloat16 [8192, 2048], P(('dp', 'expert')), may hold values from -6 to 6
- cotangent: bfloat16 [8192, 2048], P(('dp', 'expert')), may hold values from -6 to 6
- expert_ids: int32 [8192, 8], P(('dp', 'expert')), may hold values from 0 to 127, all different within a row; in each aligned block of 16 rows (0 to 15, 16 to 31, ...) at most 2 rows name the same one
- gate_values: float32 [8192, 8], P(('dp', 'expert')), may hold values from 0.05 to 0.5
- gate_weight: bfloat16 [128, 2048, 384], P('expert', 'dp'), may hold values from -0.125 to 0.125
- up_weight: bfloat16 [128, 2048, 384], P('expert', 'dp'), may hold values from -0.125 to 0.125
- down_weight: bfloat16 [128, 2048, 384], P('expert', 'dp'), may hold values from -0.3125 to 0.3125
Outputs:
- mixed: bfloat16 [8192, 2048], P(('dp', 'expert'))
- input_grad: bfloat16 [8192, 2048], P(('dp', 'expert'))
- gate_grad: float32 [8192, 8], P(('dp', 'expert'))
- gate_weight_grad: float32 [128, 2048, 384], P('expert', 'dp')
- up_weight_grad: float32 [128, 2048, 384], P('expert', 'dp')
The draws below stay inside these ranges and needn't reach their ends.
Inputs may be any that keep to these rules, and one draw needn't show every extreme that they name: `expert_ids`: each row names 8 different experts. Among the 16 rows of one device no expert is named more than 2 times.
All inputs are finite; a program needn't handle non-finite values.
Results may differ from the reference program's by a relative error of at most 0.012.
Values may be sent and summed in bfloat16 or wider, within the bound.
A program may use at most 64 MiB of HBM per device.

```python
import math
import jax
import jax.numpy as jnp
import numpy as np
from jax import lax

D = 2048
H = 384
TOP = 8
TOK_DEV = 16
EXPERTS = 128
TOKENS = 8192
CAP = 2
N_DP = 4
N_EXPERT = 128


def level_of(own_key, shape, split, smallest, top_value):
    level = 1.0
    for dim, shards_of in split:
        steps = jax.random.uniform(jax.random.fold_in(jax.random.fold_in(own_key, 6), dim), (shards_of,), jnp.float32, smallest / len(split), top_value / len(split))
        level = level * jnp.repeat(jnp.exp(steps), shape[dim] // shards_of).reshape((-1,) + (1,) * (len(shape) - 1 - dim))
    return level


def routed_block(stream_key, own, number, rows, amount, top, bound, slope):
    ranking = jax.random.permutation(stream_key, amount)
    packed, common = portions_of(amount, rows * top, bound, slope, True), portions_of(amount, rows * top, bound, slope, False)
    places = jnp.arange(amount)

    def named(tallies, turn):
        used = int((tallies > 0).sum())
        fixed = max(1, used // 4)
        passed = fixed + (places - fixed + turn * (used - fixed)) % max(1, amount - fixed)
        return jnp.zeros((amount,), jnp.int32).at[ranking[jnp.where(places < fixed, places, passed)]].set(jnp.asarray(tallies, jnp.int32))

    tallies = jnp.where(number % 4 == 0, named(packed, number // 4), named(common, number - number // 4 - 1))
    mixed = jax.random.permutation(jax.random.fold_in(own, 3), amount)
    giver, receiver = mixed[0:amount // 2 * 2:2], mixed[1:amount // 2 * 2:2]
    room = jnp.minimum(tallies[giver] - 1, bound - tallies[receiver]) // 2
    room = jnp.where((giver == ranking[0]) | (receiver == ranking[0]) | (tallies[receiver] == 0), 0, jnp.maximum(room, 0))
    passed = jax.random.randint(jax.random.fold_in(own, 4), (amount // 2,), 0, 1 << 20) % (room + 1)
    tallies = tallies.at[giver].add(-passed).at[receiver].add(passed)
    labels = jnp.searchsorted(jnp.cumsum(tallies), jnp.arange(rows * top), side="right").astype(jnp.int32)
    listing = labels.reshape(top, rows).T
    listing = listing[jax.random.permutation(jax.random.fold_in(own, 1), rows)]
    turn = jax.random.randint(jax.random.fold_in(own, 2), (rows, 1), 0, top)
    return jnp.take_along_axis(listing, (jnp.arange(top)[None, :] + turn) % top, axis=1)


def portions_of(number_of, total, bound, slope, full):
    loads = [(1 << 20) // math.isqrt(standing ** slope) + 1 for standing in range(1, number_of + 1)]
    largest = bound if full else min(bound, max(-(-total // number_of), total * loads[0] // sum(loads)))
    least = 1 if total - largest >= number_of - 1 else 0
    given, rest = [largest] + [least] * (number_of - 1), total - largest - least * (number_of - 1)
    while rest > 0:
        free = [i for i in range(1, number_of) if given[i] < largest] or [i for i in range(1, number_of) if given[i] < bound]
        mass, left = sum([loads[i] for i in free]), rest
        for i in free:
            extra = min(bound - given[i], max(1, left * loads[i] // mass), rest)
            given[i] = given[i] + extra
            rest = rest - extra
    return np.array(given)


def normal_values(key, dims, scale, reach, cuts=(), held_as=jnp.bfloat16):
    gain = level_of(key, dims, cuts, -0.22, 0.18) if cuts else 1.0
    result = jax.random.normal(key, dims, jnp.float32) * scale * gain
    return jnp.minimum(jnp.maximum(result, -reach), reach).astype(held_as)


def setup_inputs(seed: int = 0) -> dict:
    splits = jax.random.split(jax.random.key(seed), 8)
    tokens = normal_values(splits[0], (TOKENS, D), 1.0, 6.0, ((0, 512),))
    cotangent = normal_values(splits[1], (TOKENS, D), 1.0, 6.0, ((0, 512),))
    expert_ids_keys = jax.random.split(jax.random.fold_in(splits[2], 1), TOKENS // TOK_DEV)
    expert_ids_turns = jax.random.permutation(jax.random.fold_in(splits[2], 3), TOKENS // TOK_DEV)
    expert_ids = jax.vmap(lambda own, number: routed_block(jax.random.fold_in(splits[2], 2), own, number, TOK_DEV, EXPERTS, TOP, CAP, 2))(expert_ids_keys, expert_ids_turns).reshape((TOKENS, TOP))
    gate_values = jnp.clip(jnp.exp(math.log(0.5) - 2.3025851 * jax.random.uniform(splits[3], (TOKENS, TOP), jnp.float32) ** level_of(splits[3], (TOKENS, TOP), ((0, 512),), -0.2, 0.2)), 0.05, 0.5)
    gate_weight = normal_values(splits[4], (EXPERTS, D, H), D ** -0.5, 0.125, ((0, 128), (1, 4)))
    up_weight = normal_values(splits[5], (EXPERTS, D, H), D ** -0.5, 0.125, ((0, 128), (1, 4)))
    down_weight = normal_values(splits[6], (EXPERTS, D, H), H ** -0.5, 0.3125, ((0, 128), (1, 4)))
    return dict(tokens=tokens, cotangent=cotangent, expert_ids=expert_ids, gate_values=gate_values, gate_weight=gate_weight, up_weight=up_weight, down_weight=down_weight)


def expert_pass(rows, grad_rows, gate_mat, up_mat, down_mat):
    hidden_gate = jnp.dot(rows, gate_mat, preferred_element_type=jnp.float32)
    hidden_up = jnp.dot(rows, up_mat, preferred_element_type=jnp.float32)
    sigma = jax.nn.sigmoid(hidden_gate)
    active = (hidden_gate * sigma * hidden_up).astype(jnp.bfloat16)
    outputs = jnp.dot(active, down_mat.T, preferred_element_type=jnp.float32).astype(jnp.bfloat16)
    grad_active = jnp.dot(grad_rows, down_mat, preferred_element_type=jnp.float32)
    grad_up = (grad_active * hidden_gate * sigma).astype(jnp.bfloat16)
    grad_gate = (grad_active * hidden_up * sigma * (1.0 + hidden_gate * (1.0 - sigma))).astype(jnp.bfloat16)
    input_rows = jnp.dot(grad_gate, gate_mat.T, preferred_element_type=jnp.float32)
    input_rows = (input_rows + jnp.dot(grad_up, up_mat.T, preferred_element_type=jnp.float32)).astype(jnp.bfloat16)
    gate_part = jnp.dot(rows.T, grad_gate, preferred_element_type=jnp.float32)
    up_part = jnp.dot(rows.T, grad_up, preferred_element_type=jnp.float32)
    return outputs, input_rows, gate_part, up_part


def reference(tokens, cotangent, expert_ids, gate_values, gate_weight, up_weight, down_weight):
    blocks = N_DP * N_EXPERT
    routed = TOK_DEV * TOP
    total_pairs = TOKENS * TOP
    ids_block = expert_ids.reshape(blocks, routed)
    onehot = (ids_block[:, :, None] == jnp.arange(EXPERTS, dtype=jnp.int32)[None, None, :]).astype(jnp.int32)
    earlier = jnp.cumsum(onehot, axis=1) - onehot
    slot_rank = jnp.sum(earlier * onehot, axis=2).astype(jnp.int32)
    block_index = jnp.arange(blocks, dtype=jnp.int32)[:, None]
    group_index = block_index // N_EXPERT
    source_index = block_index % N_EXPERT
    position = ((group_index * EXPERTS + ids_block) * N_EXPERT + source_index) * CAP + slot_rank
    pair_index = block_index * routed + jnp.arange(routed, dtype=jnp.int32)[None, :]
    slot_pair = jnp.full((N_DP * EXPERTS * N_EXPERT * CAP,), total_pairs, jnp.int32)
    slot_pair = slot_pair.at[position.reshape(-1)].set(pair_index.reshape(-1).astype(jnp.int32))
    slot_pair = slot_pair.reshape(N_DP, EXPERTS, N_EXPERT * CAP).transpose(1, 0, 2)
    tokens_ext = jnp.concatenate([tokens, jnp.zeros((1, D), jnp.bfloat16)], axis=0)
    cot_ext = jnp.concatenate([cotangent.astype(jnp.float32), jnp.zeros((1, D), jnp.float32)], axis=0)
    gate_ext = jnp.concatenate([gate_values.reshape(-1), jnp.zeros((1,), jnp.float32)], axis=0)

    def expert_step(carry, inputs):
        mixed_acc, input_acc, gate_acc = carry
        pairs, gate_mat, up_mat, down_mat = inputs
        gate_sum = jnp.zeros((D, H), jnp.float32)
        up_sum = jnp.zeros((D, H), jnp.float32)
        for group in range(N_DP):
            pair_row = pairs[group]
            token_row = (pair_row // TOP).astype(jnp.int32)
            rows = tokens_ext[token_row]
            weight_row = gate_ext[pair_row]
            grad_rows = (weight_row[:, None] * cot_ext[token_row]).astype(jnp.bfloat16)
            outputs, input_rows, gate_part, up_part = expert_pass(rows, grad_rows, gate_mat, up_mat, down_mat)
            mixed_acc = mixed_acc.at[token_row].add(weight_row[:, None] * outputs.astype(jnp.float32))
            input_acc = input_acc.at[token_row].add(input_rows.astype(jnp.float32))
            gate_acc = gate_acc.at[pair_row].set(jnp.sum(outputs.astype(jnp.float32) * cot_ext[token_row], axis=1))
            gate_sum = gate_sum + lax.optimization_barrier(gate_part.astype(jnp.bfloat16)).astype(jnp.float32)
            up_sum = up_sum + lax.optimization_barrier(up_part.astype(jnp.bfloat16)).astype(jnp.float32)
        return (mixed_acc, input_acc, gate_acc), (gate_sum, up_sum)

    start = (jnp.zeros((TOKENS + 1, D), jnp.float32), jnp.zeros((TOKENS + 1, D), jnp.float32), jnp.zeros((total_pairs + 1,), jnp.float32))
    final, grads = lax.scan(expert_step, start, (slot_pair, gate_weight, up_weight, down_weight))
    mixed_acc, input_acc, gate_acc = final
    mixed = mixed_acc[:TOKENS].astype(jnp.bfloat16)
    input_grad = input_acc[:TOKENS].astype(jnp.bfloat16)
    gate_grad = gate_acc[:total_pairs].reshape(TOKENS, TOP)
    return mixed, input_grad, gate_grad, grads[0], grads[1]
```

```python
import functools

import jax
import jax.numpy as jnp
from jax import lax
from jax.experimental import pallas as pl
from jax.experimental.pallas import tpu as pltpu
from jax.sharding import PartitionSpec as P

MESH = pl.DeviceIdType.MESH
NX, NZ, NJ = 4, 16, 8
TOK, D, H, TOP = 16, 2048, 384, 8
NB = 8
ROWS = NB * TOK
COLS = 512
F32, BF16 = jnp.float32, jnp.bfloat16
NT = (((1,), (1,)), ((), ()))


def dot(a, b):
    return jnp.dot(a, b, preferred_element_type=F32)


def dot_t(a, b):
    return lax.dot_general(a, b, NT, preferred_element_type=F32)


def iota(shape, dim):
    return lax.broadcasted_iota(jnp.int32, shape, dim)


def halves(v):
    hi = v.astype(BF16)
    return hi, (v - hi.astype(F32)).astype(BF16)


def kernel(
    tok_ref, cot_ref, meta_ref, gw_ref, uw_ref, dw_ref,
    mixed_ref, igrad_ref, gg_ref, ggw_ref, guw_ref,
    W, AG, MT, STG, ROW, PCOT, XT, HG, HU, ACT, DGU, OST, RET, PART, RSS, RSR, PS, PR, GGS, GGR, ONE, TG, EX,
    w_s, w_r, l_s, ag_s, ag_r, mt_s, mt_r, di_s, di_r, re_s, re_r, rs_s, rs_r, p_s, p_r, gg_s, gg_r,
):
    x = lax.axis_index("dp")
    e = lax.axis_index("expert")
    z = e // NJ
    j = lax.rem(e, NJ)

    def zpeer(d):
        return {"dp": x, "expert": lax.rem(z + d + NZ, NZ) * NJ + j}

    def jat(q):
        return lax.rem(j + q + NJ, NJ)

    def xat(q):
        return lax.rem(x + q + NX, NX)

    def jpeer(q):
        return {"dp": x, "expert": z * NJ + jat(q)}

    def xpeer(q):
        return {"dp": xat(q), "expert": e}

    barrier = pltpu.get_barrier_semaphore()
    peers = [zpeer(d) for d in range(1, NZ)] + [jpeer(q) for q in range(1, NJ)] + [xpeer(q) for q in range(1, NX)]
    for peer in peers:
        pl.semaphore_signal(barrier, inc=1, device_id=peer, device_id_type=MESH)
    pl.semaphore_wait(barrier, len(peers))

    sent = []

    def send(src, dst, s, r, peer):
        copy = pltpu.make_async_remote_copy(
            src_ref=src, dst_ref=dst, send_sem=s, recv_sem=r, device_id=peer, device_id_type=MESH
        )
        copy.start()
        sent.append(copy)
        return copy

    arrive = {}

    def ag_send(tc, r, step):
        to = (r - step) % NZ
        src = (tok_ref, cot_ref)[tc] if r == 4 else AG.at[tc, r]
        arrive[tc, to] = send(src, AG.at[tc, to], ag_s.at[tc, to], ag_r.at[tc, to], zpeer(step))

    for tc in (0, 1):
        ag_send(tc, 4, 8)
        ag_send(tc, 4, 1)
        ag_send(tc, 4, -1)
        if tc == 0:
            meta = [
                send(meta_ref, MT.at[(4 - d) % NZ], mt_s.at[d], mt_r.at[d], zpeer(d)) for d in range(1, NZ)
            ]
    own = []
    weights = {}
    for i, ref in enumerate((gw_ref, uw_ref, dw_ref)):
        for q in (2, 1, 3):
            weights[i, q] = send(ref.at[0], W.at[i, x], w_s.at[i, q], w_r.at[i, q], xpeer(q))
        copy = pltpu.make_async_copy(ref.at[0], W.at[i, x], l_s.at[i])
        copy.start()
        own.append(copy)
    MT[4] = meta_ref[...]
    AG[0, 4] = tok_ref[...]
    AG[1, 4] = cot_ref[...]

    def hop(base, h):
        for tc in (0, 1):
            if h == 0:
                if base == 12:
                    arrive[tc, 12].wait_recv()
                    ag_send(tc, 12, 1)
                    ag_send(tc, 12, -1)
                continue
            arrive[tc, base - h].wait_recv()
            if h < 4:
                ag_send(tc, base - h, 1)
                arrive[tc, base + h].wait_recv()
                if h < 3:
                    ag_send(tc, base + h, -1)

    def select(ch):
        m = MT[pl.ds(NB * ch, NB)].reshape(NB * 8, 128).astype(BF16)
        row, col = iota((ROWS, NB * 8), 0), iota((ROWS, NB * 8), 1)
        mine = lax.rem(row, 16) // 2 * 8
        codes = dot((col == mine).astype(F32).astype(BF16), m)
        gates = dot(((col == mine + 1) | (col == mine + 2)).astype(F32).astype(BF16), m)
        row = iota((ROWS, 128), 0)
        col = iota((ROWS, 128), 1)
        want = ((z * NJ + row // 16) * 2 + lax.rem(row, 2)).astype(F32)
        taken = (codes == want).astype(F32)
        gate = jnp.sum(taken * gates, axis=1, keepdims=True)
        fold = (row // TOP == lax.rem(col, TOK)).astype(F32).astype(BF16)
        one = dot(taken.astype(BF16), fold)
        one = jnp.where(lax.rem(row, 16) // 2 == col // TOK, one, 0.0)
        EX[ch] = taken.astype(BF16)
        ONE[ch] = one.astype(BF16)
        one_t = one.T
        TG[ch, 0] = one_t.astype(BF16)
        gated = (one * gate).T
        hi, lo = halves(gated)
        TG[ch, 1] = hi
        TG[ch, 2] = lo
        return gate

    rows_in = {}

    def pack(ch, gate):
        one = ONE[ch]

        @pl.loop(0, D // COLS)
        def _(n):
            at = pl.ds(pl.multiple_of(n * COLS, COLS), COLS)
            block = AG[0, pl.ds(NB * ch, NB), :, at].reshape(ROWS, COLS)
            STG[ch, 0, :, :, at] = dot(one, block).astype(BF16).reshape(NJ, 16, COLS)
            block = AG[1, pl.ds(NB * ch, NB), :, at].reshape(ROWS, COLS)
            picked = dot(one, block)
            PCOT[ch, :, at] = picked.astype(BF16)
            STG[ch, 1, :, :, at] = (picked * gate).astype(BF16).reshape(NJ, 16, COLS)

        for tc in (0, 1):
            for q in range(1, NJ):
                rows_in[ch, tc, q] = send(
                    STG.at[ch, tc, jat(q)], ROW.at[tc, ch, j], di_s.at[ch, tc, q], di_r.at[ch, tc, q], jpeer(q)
                )
            ROW[tc, ch, j] = STG[ch, tc, j]

    hop(4, 1)
    hop(12, 0)
    hop(4, 2)
    for copy in meta:
        copy.wait_recv()
    gate_a = select(0)
    hop(12, 1)
    hop(4, 3)
    gate_b = select(1)
    hop(12, 2)
    hop(4, 4)
    hop(12, 3)
    pack(0, gate_a)
    hop(12, 4)
    pack(1, gate_b)
    for ch in (0, 1):
        for tc in (0, 1):
            for q in range(1, NJ):
                rows_in[ch, tc, q].wait_recv()

    @pl.loop(0, D // COLS)
    def _(n):
        at = pl.ds(pl.multiple_of(n * COLS, COLS), COLS)
        XT[at, :] = ROW[0, :, :, :, at].reshape(2 * ROWS, COLS).T

    def weight_in(i):
        own[i].wait()
        for q in range(1, NX):
            weights[i, q].wait_recv()

    def rows_by(i, tc, to):
        to[...] = jnp.zeros_like(to)

        @pl.loop(0, NX)
        def _(n):
            at = pl.ds(pl.multiple_of(n * COLS, COLS), COLS)
            to[...] += dot(ROW[tc, :, :, :, at].reshape(2 * ROWS, COLS), W[i, n])

    weight_in(0)
    rows_by(0, 0, HG)
    weight_in(1)
    rows_by(1, 0, HU)
    hg, hu = HG[...], HU[...]
    sigma = jax.nn.sigmoid(hg)
    ACT[...] = (hg * sigma * hu).astype(BF16)
    weight_in(2)

    back = {}

    def give_back(arr):
        for ch in (1, 0):
            for q in range(1, NJ):
                back[arr, ch, q] = send(
                    OST.at[arr, ch, jat(q)], RET.at[arr, ch, j], re_s.at[arr, ch, q], re_r.at[arr, ch, q], jpeer(q)
                )
            RET[arr, ch, j] = OST[arr, ch, j]

    @pl.loop(0, NX)
    def _(n):
        at = pl.ds(pl.multiple_of(n * COLS, COLS), COLS)
        OST[0, :, :, :, at] = dot_t(ACT[...], W[2, n]).astype(BF16).reshape(2, NJ, 16, COLS)

    give_back(0)
    rows_by(2, 1, HU)
    da = HU[...]
    DGU[1] = (da * hg * sigma).astype(BF16)
    DGU[0] = (da * hu * sigma * (1.0 + hg * (1.0 - sigma))).astype(BF16)

    @pl.loop(0, NX)
    def _(n):
        at = pl.ds(pl.multiple_of(n * COLS, COLS), COLS)
        dx = dot_t(DGU[0], W[0, n]) + dot_t(DGU[1], W[1, n])
        OST[1, :, :, :, at] = dx.astype(BF16).reshape(2, NJ, 16, COLS)

    give_back(1)

    @pl.loop(0, NX)
    def _(n):
        at = pl.ds(pl.multiple_of(n * COLS, COLS), COLS)
        PS[0, n] = dot(XT[at, :], DGU[0]).astype(BF16)
        PS[1, n] = dot(XT[at, :], DGU[1]).astype(BF16)

    parts = [
        send(PS.at[arr, xat(q)], PR.at[arr, q], p_s.at[arr, q], p_r.at[arr, q], xpeer(q))
        for arr in (0, 1)
        for q in (2, 1, 3)
    ]

    def combine(arr, ch):
        for q in range(1, NJ):
            back[arr, ch, q].wait_recv()

        def step(n, dots):
            at = pl.ds(pl.multiple_of(n * COLS, COLS), COLS)
            block = RET[arr, ch, :, :, at].reshape(ROWS, COLS)
            if arr == 0:
                part = dot(TG[ch, 1], block) + dot(TG[ch, 2], block)
                dots = dots + jnp.sum(block.astype(F32) * PCOT[ch, :, at].astype(F32), axis=1, keepdims=True)
            else:
                part = dot(TG[ch, 0], block)
            PART[arr, pl.ds(NB * ch, NB), :, at] = part.reshape(NB, TOK, COLS)
            return dots

        return lax.fori_loop(0, D // COLS, step, jnp.zeros((ROWS, 1), F32))

    arrived = {}

    def rs_send(arr, r, step, to, value):
        RSS[arr, r] = value.astype(BF16)
        arrived[arr, to] = send(RSS.at[arr, r], RSR.at[arr, to], rs_s.at[arr, to], rs_r.at[arr, to], zpeer(step))

    def rs_take(arr, r):
        arrived[arr, r].wait_recv()
        return RSR[arr, r].astype(F32)

    def rs_start(arr, base):
        rs_send(arr, base - 4, -1, base - 3, PART[arr, base - 4])
        rs_send(arr, base + 3, 1, base + 2, PART[arr, base + 3])

    def rs_hop(arr, base, h):
        r = base - 4 + h
        rs_send(arr, r, -1, r + 1, PART[arr, r] + rs_take(arr, r))
        if h < 3:
            r = base + 3 - h
            to = r - 1 if h < 2 else base + 3
            rs_send(arr, r, 1, to, PART[arr, r] + rs_take(arr, r))

    def rs_sum(arr, base):
        return PART[arr, base] + rs_take(arr, base) + rs_take(arr, base + 3)

    gg = {}

    def gates_back(ch, dots):
        taken = EX[ch].astype(F32)
        row, col = iota((NB * 8, ROWS), 0), iota((NB * 8, ROWS), 1)
        pick = (row == lax.rem(col, 16) // 2 * 8).astype(F32).astype(BF16)
        hi, lo = halves(taken * dots)
        GGS[pl.ds(NB * ch, NB)] = (dot(pick, hi) + dot(pick, lo)).reshape(NB, 8, 128)
        for r in range(NB * ch, NB * ch + NB):
            if r != 4:
                d = (r - 4) % NZ
                gg[d] = send(GGS.at[r], GGR.at[d], gg_s.at[d], gg_r.at[d], zpeer(d))

    for arr in (0, 1):
        for ch in (1, 0):
            dots = combine(arr, ch)
            rs_start(arr, 4 + NB * ch)
            if arr == 0:
                gates_back(ch, dots)
    for h in (1, 2, 3):
        for base in (12, 4):
            for arr in (0, 1):
                rs_hop(arr, base, h)
    for arr in (0, 1):
        rs_send(arr, 12, 8, 0, rs_sum(arr, 12))
    for copy in parts:
        copy.wait_recv()
    for arr, ref in ((0, ggw_ref), (1, guw_ref)):
        total = PS[arr, x].astype(F32)
        for q in range(1, NX):
            total = total + PR[arr, q].astype(F32)
        ref[0] = total
    total = GGS[4]
    for d in range(1, NZ):
        gg[d].wait_recv()
        total = total + GGR[d]
    gg_ref[...] = total
    for arr, ref in ((0, mixed_ref), (1, igrad_ref)):
        ref[...] = (rs_sum(arr, 4) + rs_take(arr, 0)).astype(BF16)
    for copy in sent:
        copy.wait_send()


def body(tokens, cotangent, expert_ids, gate_values, gate_weight, up_weight, down_weight):
    flat = expert_ids.reshape(1, TOK * TOP)
    route = jnp.arange(TOK * TOP)
    same = (flat.reshape(TOK * TOP, 1) == flat) & (route[:, None] < route[None, :])
    rank = jnp.sum(same.astype(jnp.int32), axis=0, keepdims=True)
    code = (flat * 2 + rank).astype(F32)
    gates = gate_values.reshape(1, TOK * TOP)
    hi = lax.reduce_precision(gates, 8, 7)
    meta = jnp.concatenate([code, hi, gates - hi, jnp.zeros((5, TOK * TOP), F32)], axis=0)

    vmem = pl.BlockSpec(memory_space=pltpu.VMEM)
    hbm = pl.BlockSpec(memory_space=pl.ANY)
    dma = pltpu.SemaphoreType.DMA
    v = pltpu.VMEM
    outs = (
        jax.ShapeDtypeStruct((TOK, D), BF16),
        jax.ShapeDtypeStruct((TOK, D), BF16),
        jax.ShapeDtypeStruct((8, 128), F32),
        jax.ShapeDtypeStruct((1, COLS, H), F32),
        jax.ShapeDtypeStruct((1, COLS, H), F32),
    )
    mixed, igrad, gg, ggw, guw = pl.pallas_call(
        kernel,
        out_shape=outs,
        in_specs=[vmem] * 3 + [hbm] * 3,
        out_specs=[vmem] * 5,
        scratch_shapes=[
            v((3, NX, COLS, H), BF16),
            v((2, NZ, TOK, D), BF16),
            v((NZ, 8, 128), F32),
            v((2, 2, NJ, 16, D), BF16),
            v((2, 2, NJ, 16, D), BF16),
            v((2, ROWS, D), BF16),
            v((D, 2 * ROWS), BF16),
            v((2 * ROWS, H), F32),
            v((2 * ROWS, H), F32),
            v((2 * ROWS, H), BF16),
            v((2, 2 * ROWS, H), BF16),
            v((2, 2, NJ, 16, D), BF16),
            v((2, 2, NJ, 16, D), BF16),
            v((2, NZ, TOK, D), F32),
            v((2, NZ, TOK, D), BF16),
            v((2, NZ, TOK, D), BF16),
            v((2, NX, COLS, H), BF16),
            v((2, NX, COLS, H), BF16),
            v((NZ, 8, 128), F32),
            v((NZ, 8, 128), F32),
            v((2, ROWS, ROWS), BF16),
            v((2, 3, ROWS, ROWS), BF16),
            v((2, ROWS, 128), BF16),
            dma((3, NX)), dma((3, NX)), dma((3,)),
            dma((2, NZ)), dma((2, NZ)),
            dma((NZ,)), dma((NZ,)),
            dma((2, 2, NJ)), dma((2, 2, NJ)),
            dma((2, 2, NJ)), dma((2, 2, NJ)),
            dma((2, NZ)), dma((2, NZ)),
            dma((2, NX)), dma((2, NX)),
            dma((NZ,)), dma((NZ,)),
        ],
        compiler_params=pltpu.CompilerParams(
            collective_id=0, has_side_effects=True, vmem_limit_bytes=48 * 2**20
        ),
        name="experts",
    )(tokens, cotangent, meta, gate_weight, up_weight, down_weight)
    return mixed, igrad, gg[0].reshape(TOK, TOP), ggw, guw


def solution(mesh):
    token = P(("dp", "expert"), None)
    weight = P("expert", "dp", None)
    return jax.shard_map(
        body,
        mesh=mesh,
        in_specs=(token,) * 4 + (weight,) * 3,
        out_specs=(token,) * 3 + (weight,) * 2,
        check_vma=False,
    )
```

```python
import functools

import jax
import jax.numpy as jnp
from jax import lax
from jax.experimental import pallas as pl
from jax.experimental.pallas import tpu as pltpu
from jax.sharding import PartitionSpec as P

MESH = pl.DeviceIdType.MESH
NX, NZ, NJ = 4, 16, 8
TOK, D, H, TOP = 16, 2048, 384, 8
NB = 8
ROWS = NB * TOK
COLS = 512
WIDE = D + 128
F32, BF16 = jnp.float32, jnp.bfloat16
NT = (((1,), (1,)), ((), ()))


def dot(a, b):
    return jnp.dot(a, b, preferred_element_type=F32)


def dot_t(a, b):
    return lax.dot_general(a, b, NT, preferred_element_type=F32)


def iota(shape, dim):
    return lax.broadcasted_iota(jnp.int32, shape, dim)


def halves(v):
    hi = v.astype(BF16)
    return hi, (v - hi.astype(F32)).astype(BF16)


def kernel(
    tok_ref, cot_ref, meta_ref, gw_ref, uw_ref, dw_ref,
    mixed_ref, igrad_ref, gg_ref, ggw_ref, guw_ref,
    W, AGT, AGC, STG, ROW, PCOT, XT, HG, HU, ACT, DGU, OST, RET, PARTM, PARTX, RSSM, RSSX, RSRM, RSRX, PS, PR, ONE, TG, EX,
    w_s, w_r, l_s, ag_s, ag_r, di_s, di_r, re_s, re_r, rs_s, rs_r, p_s, p_r,
):
    x = lax.axis_index("dp")
    e = lax.axis_index("expert")
    z = e // NJ
    j = lax.rem(e, NJ)

    def zpeer(d):
        return {"dp": x, "expert": lax.rem(z + d + NZ, NZ) * NJ + j}

    def jat(q):
        return lax.rem(j + q + NJ, NJ)

    def xat(q):
        return lax.rem(x + q + NX, NX)

    def jpeer(q):
        return {"dp": x, "expert": z * NJ + jat(q)}

    def xpeer(q):
        return {"dp": xat(q), "expert": e}

    barrier = pltpu.get_barrier_semaphore()
    peers = [zpeer(d) for d in (1, -1, 2, -2)] + [jpeer(q) for q in range(1, NJ)] + [xpeer(q) for q in range(1, NX)]
    for peer in peers:
        pl.semaphore_signal(barrier, inc=1, device_id=peer, device_id_type=MESH)
    pl.semaphore_wait(barrier, len(peers))

    sent = []

    def send(src, dst, s, r, peer):
        copy = pltpu.make_async_remote_copy(
            src_ref=src, dst_ref=dst, send_sem=s, recv_sem=r, device_id=peer, device_id_type=MESH
        )
        copy.start()
        sent.append(copy)
        return copy

    AG = (AGT, AGC)
    arrive = {}

    def ag_send(tc, r, *steps):
        for step in steps:
            to = (r - step) % NZ
            arrive[tc, to] = send(AG[tc].at[r], AG[tc].at[to], ag_s.at[tc, to], ag_r.at[tc, to], zpeer(step))

    def ag_stage(tc, stage):
        if stage == 0:
            ag_send(tc, 4, 2, -2, 1, -1)
            return
        r = 4 - 2 * stage
        arrive[tc, r % NZ].wait_recv()
        ag_send(tc, r % NZ, 2, 1)
        r = 4 + 2 * stage
        arrive[tc, r].wait_recv()
        ag_send(tc, r, *((-2, -1) if stage < 3 else (-1,)))

    def ag_wait(tc, *places):
        for r in places:
            arrive[tc, r].wait_recv()

    AGT[4, :, :D] = tok_ref[...]
    AGT[4, :, D:] = meta_ref[...]
    AGC[4] = cot_ref[...]
    ag_stage(0, 0)

    HALF = COLS // 2
    own = []
    weights = {}
    relays = {}
    for i, ref in enumerate((gw_ref, uw_ref, dw_ref)):
        for q in (1, 3):
            weights[i, q] = send(ref.at[0], W.at[i, x], w_s.at[i, q], w_r.at[i, q], xpeer(q))
        copy = pltpu.make_async_copy(ref.at[0], W.at[i, x], l_s.at[i])
        copy.start()
        own.append(copy)

    def relay(i):
        for q, half in ((1, 0), (3, 1)):
            weights[i, q].wait_recv()
            block = W.at[i, xat(-q), pl.ds(half * HALF, HALF)]
            relays[i, half] = send(block, block, w_s.at[i, 2 * half], w_r.at[i, 2 * half], xpeer(q))

    def select(ch):
        m = AGT[pl.ds(NB * ch, NB), :, D:].reshape(ROWS, 128)
        row, col = iota((ROWS, ROWS), 0), iota((ROWS, ROWS), 1)
        mine = lax.rem(row, 16) // 2 * TOK
        codes = dot((col == mine).astype(F32).astype(BF16), m)
        gates = dot(((col == mine + 1) | (col == mine + 2)).astype(F32).astype(BF16), m)
        row = iota((ROWS, 128), 0)
        col = iota((ROWS, 128), 1)
        want = ((z * NJ + row // 16) * 2 + lax.rem(row, 2)).astype(F32)
        taken = (codes == want).astype(F32)
        gate = jnp.sum(taken * gates, axis=1, keepdims=True)
        fold = (row // TOP == lax.rem(col, TOK)).astype(F32).astype(BF16)
        one = dot(taken.astype(BF16), fold)
        one = jnp.where(lax.rem(row, 16) // 2 == col // TOK, one, 0.0)
        EX[ch] = taken.astype(BF16)
        ONE[ch] = one.astype(BF16)
        one_t = one.T
        TG[ch, 0] = one_t.astype(BF16)
        gated = (one * gate).T
        hi, lo = halves(gated)
        TG[ch, 1] = hi
        TG[ch, 2] = lo
        return gate

    rows_in = {}

    def pack(tc, ch, gate):
        one = ONE[ch]

        @pl.loop(0, D // COLS)
        def _(n):
            at = pl.ds(pl.multiple_of(n * COLS, COLS), COLS)
            picked = dot(one, AG[tc][pl.ds(NB * ch, NB), :, at].reshape(ROWS, COLS))
            if tc == 1:
                PCOT[ch, :, at] = picked.astype(BF16)
                picked = picked * gate
            STG[ch, tc, :, :, at] = picked.astype(BF16).reshape(NJ, 16, COLS)

        for q in range(1, NJ):
            rows_in[ch, tc, q] = send(
                STG.at[ch, tc, jat(q)], ROW.at[tc, ch, j], di_s.at[ch, tc, q], di_r.at[ch, tc, q], jpeer(q)
            )
        ROW[tc, ch, j] = STG[ch, tc, j]

    def rows_wait(tc):
        for ch in (0, 1):
            for q in range(1, NJ):
                rows_in[ch, tc, q].wait_recv()

    ag_stage(0, 1)
    ag_stage(1, 0)
    ag_stage(0, 2)
    ag_stage(1, 1)
    ag_wait(0, 1, 3, 5, 7)
    gate_a = select(0)
    ag_stage(0, 3)
    ag_stage(1, 2)
    pack(0, 0, gate_a)
    relay(0)
    ag_wait(0, 9, 11, 12, 13, 15)
    gate_b = select(1)
    ag_stage(1, 3)
    pack(0, 1, gate_b)
    relay(1)
    ag_wait(1, 1, 3, 5, 7)
    pack(1, 0, gate_a)
    relay(2)
    ag_wait(1, 9, 11, 12, 13, 15)
    pack(1, 1, gate_b)
    rows_wait(0)

    @pl.loop(0, D // COLS)
    def _(n):
        at = pl.ds(pl.multiple_of(n * COLS, COLS), COLS)
        XT[at, :] = ROW[0, :, :, :, at].reshape(2 * ROWS, COLS).T

    def weight_in(i):
        own[i].wait()
        for half in (0, 1):
            relays[i, half].wait_recv()

    def rows_by(i, tc, to):
        to[...] = jnp.zeros_like(to)

        @pl.loop(0, NX)
        def _(n):
            at = pl.ds(pl.multiple_of(n * COLS, COLS), COLS)
            to[...] += dot(ROW[tc, :, :, :, at].reshape(2 * ROWS, COLS), W[i, n])

    weight_in(0)
    rows_by(0, 0, HG)
    weight_in(1)
    rows_by(1, 0, HU)
    hg, hu = HG[...], HU[...]
    sigma = jax.nn.sigmoid(hg)
    ACT[...] = (hg * sigma * hu).astype(BF16)
    weight_in(2)

    back = {}

    def give_back(arr):
        for ch in (1, 0):
            for q in range(1, NJ):
                back[arr, ch, q] = send(
                    OST.at[arr, ch, jat(q)], RET.at[arr, ch, j], re_s.at[arr, ch, q], re_r.at[arr, ch, q], jpeer(q)
                )
            RET[arr, ch, j] = OST[arr, ch, j]

    @pl.loop(0, NX)
    def _(n):
        at = pl.ds(pl.multiple_of(n * COLS, COLS), COLS)
        OST[0, :, :, :, at] = dot_t(ACT[...], W[2, n]).astype(BF16).reshape(2, NJ, 16, COLS)

    give_back(0)
    rows_wait(1)
    rows_by(2, 1, HU)
    da = HU[...]
    DGU[1] = (da * hg * sigma).astype(BF16)
    DGU[0] = (da * hu * sigma * (1.0 + hg * (1.0 - sigma))).astype(BF16)

    @pl.loop(0, NX)
    def _(n):
        at = pl.ds(pl.multiple_of(n * COLS, COLS), COLS)
        PS[0, n] = dot(XT[at, :], DGU[0]).astype(BF16)
        PS[1, n] = dot(XT[at, :], DGU[1]).astype(BF16)

    parts = [
        send(PS.at[arr, xat(q)], PR.at[arr, q], p_s.at[arr, q], p_r.at[arr, q], xpeer(q))
        for arr in (0, 1)
        for q in (2, 1, 3)
    ]

    @pl.loop(0, NX)
    def _(n):
        at = pl.ds(pl.multiple_of(n * COLS, COLS), COLS)
        dx = dot_t(DGU[0], W[0, n]) + dot_t(DGU[1], W[1, n])
        OST[1, :, :, :, at] = dx.astype(BF16).reshape(2, NJ, 16, COLS)

    give_back(1)

    PART, RSS, RSR = (PARTM, PARTX), (RSSM, RSSX), (RSRM, RSRX)

    def combine(arr, ch):
        for q in range(1, NJ):
            back[arr, ch, q].wait_recv()

        def step(n, dots):
            at = pl.ds(pl.multiple_of(n * COLS, COLS), COLS)
            block = RET[arr, ch, :, :, at].reshape(ROWS, COLS)
            if arr == 0:
                part = dot(TG[ch, 1], block) + dot(TG[ch, 2], block)
                dots = dots + jnp.sum(block.astype(F32) * PCOT[ch, :, at].astype(F32), axis=1, keepdims=True)
            else:
                part = dot(TG[ch, 0], block)
            PART[arr][pl.ds(NB * ch, NB), :, at] = part.reshape(NB, TOK, COLS)
            return dots

        dots = lax.fori_loop(0, D // COLS, step, jnp.zeros((ROWS, 1), F32))
        if arr == 0:
            hi, lo = halves(EX[ch].astype(F32) * dots)
            row, col = iota((ROWS, ROWS), 0), iota((ROWS, ROWS), 1)
            first = lax.rem(col, 16) // 2 * TOK
            grads = dot((row == first).astype(F32).astype(BF16), hi) + dot((row == first + 1).astype(F32).astype(BF16), lo)
            PARTM[pl.ds(NB * ch, NB), :, D:] = grads.reshape(NB, TOK, 128)

    arrived = {}

    def rs_send(arr, r, step):
        value = rs_sum(arr, r)
        RSS[arr][r] = value.astype(BF16)
        arrived[arr, r] = send(RSS[arr].at[r], RSR[arr].at[r], rs_s.at[arr, r], rs_r.at[arr, r], zpeer(step))

    takes = {14: (12, 13), 10: (11,), 0: (14, 15), 8: (10, 9), 2: (0, 1), 6: (8, 7), 4: (2, 6, 3, 5)}

    def rs_sum(arr, r):
        value = PART[arr][r]
        for other in takes.get(r, ()):
            arrived[arr, other].wait_recv()
            value = value + RSR[arr][other].astype(F32)
        return value

    def leaves(arr, ch):
        combine(arr, ch)
        for r, step in ((12, -2), (11, 1), (13, -1), (15, -1), (9, 1)) if ch else ((1, -1), (7, 1), (3, -1), (5, 1)):
            rs_send(arr, r, step)

    def inner(arr, stage):
        r = (14, 0, 2)[stage]
        rs_send(arr, r, -2)
        r = (10, 8, 6)[stage]
        rs_send(arr, r, 2)

    leaves(0, 1)
    leaves(0, 0)
    inner(0, 0)
    leaves(1, 1)
    inner(0, 1)
    leaves(1, 0)
    inner(1, 0)
    inner(0, 2)
    inner(1, 1)
    total = rs_sum(0, 4)
    mixed_ref[...] = total[:, :D].astype(BF16)
    gg_ref[...] = jnp.broadcast_to(total[0:1, D:] + total[1:2, D:], (8, 128))
    inner(1, 2)
    for copy in parts:
        copy.wait_recv()
    for arr, ref in ((0, ggw_ref), (1, guw_ref)):
        total = PS[arr, x].astype(F32)
        for q in range(1, NX):
            total = total + PR[arr, q].astype(F32)
        ref[0] = total
    igrad_ref[...] = rs_sum(1, 4).astype(BF16)
    for copy in sent:
        copy.wait_send()


def body(tokens, cotangent, expert_ids, gate_values, gate_weight, up_weight, down_weight):
    flat = expert_ids.reshape(1, TOK * TOP)
    route = jnp.arange(TOK * TOP)
    same = (flat.reshape(TOK * TOP, 1) == flat) & (route[:, None] < route[None, :])
    rank = jnp.sum(same.astype(jnp.int32), axis=0, keepdims=True)
    code = (flat * 2 + rank).astype(F32)
    gates = gate_values.reshape(1, TOK * TOP)
    hi = lax.reduce_precision(gates, 8, 7)
    meta = jnp.concatenate([code, hi, gates - hi, jnp.zeros((13, TOK * TOP), F32)], axis=0).astype(BF16)

    vmem = pl.BlockSpec(memory_space=pltpu.VMEM)
    hbm = pl.BlockSpec(memory_space=pltpu.HBM)
    dma = pltpu.SemaphoreType.DMA
    v = pltpu.VMEM
    outs = (
        jax.ShapeDtypeStruct((TOK, D), BF16),
        jax.ShapeDtypeStruct((TOK, D), BF16),
        jax.ShapeDtypeStruct((8, 128), F32),
        jax.ShapeDtypeStruct((1, COLS, H), F32),
        jax.ShapeDtypeStruct((1, COLS, H), F32),
    )
    mixed, igrad, gg, ggw, guw = pl.pallas_call(
        kernel,
        out_shape=outs,
        in_specs=[vmem] * 3 + [hbm] * 3,
        out_specs=[vmem] * 5,
        scratch_shapes=[
            v((3, NX, COLS, H), BF16),
            v((NZ, TOK, WIDE), BF16),
            v((NZ, TOK, D), BF16),
            v((2, 2, NJ, 16, D), BF16),
            v((2, 2, NJ, 16, D), BF16),
            v((2, ROWS, D), BF16),
            v((D, 2 * ROWS), BF16),
            v((2 * ROWS, H), F32),
            v((2 * ROWS, H), F32),
            v((2 * ROWS, H), BF16),
            v((2, 2 * ROWS, H), BF16),
            v((2, 2, NJ, 16, D), BF16),
            v((2, 2, NJ, 16, D), BF16),
            v((NZ, TOK, WIDE), F32),
            v((NZ, TOK, D), F32),
            v((NZ, TOK, WIDE), BF16),
            v((NZ, TOK, D), BF16),
            v((NZ, TOK, WIDE), BF16),
            v((NZ, TOK, D), BF16),
            v((2, NX, COLS, H), BF16),
            v((2, NX, COLS, H), BF16),
            v((2, ROWS, ROWS), BF16),
            v((2, 3, ROWS, ROWS), BF16),
            v((2, ROWS, 128), BF16),
            dma((3, NX)), dma((3, NX)), dma((3,)),
            dma((2, NZ)), dma((2, NZ)),
            dma((2, 2, NJ)), dma((2, 2, NJ)),
            dma((2, 2, NJ)), dma((2, 2, NJ)),
            dma((2, NZ)), dma((2, NZ)),
            dma((2, NX)), dma((2, NX)),
        ],
        compiler_params=pltpu.CompilerParams(
            collective_id=0, has_side_effects=True, vmem_limit_bytes=48 * 2**20
        ),
        name="experts",
    )(tokens, cotangent, meta, gate_weight, up_weight, down_weight)
    return mixed, igrad, gg[0].reshape(TOK, TOP), ggw, guw


def solution(mesh):
    token = P(("dp", "expert"), None)
    weight = P("expert", "dp", None)
    return jax.shard_map(
        body,
        mesh=mesh,
        in_specs=(token,) * 4 + (weight,) * 3,
        out_specs=(token,) * 3 + (weight,) * 2,
        check_vma=False,
    )
```

```python
import functools

import jax
import jax.numpy as jnp
from jax import lax
from jax.experimental import pallas as pl
from jax.experimental.pallas import tpu as pltpu
from jax.sharding import PartitionSpec as P

MESH = pl.DeviceIdType.MESH
NX, NZ, NJ = 4, 16, 8
TOK, D, H, TOP = 16, 2048, 384, 8
NB = 8
ROWS = NB * TOK
COLS = 512
WIDE = D + 128
F32, BF16 = jnp.float32, jnp.bfloat16
NT = (((1,), (1,)), ((), ()))


def dot(a, b):
    return jnp.dot(a, b, preferred_element_type=F32)


def dot_t(a, b):
    return lax.dot_general(a, b, NT, preferred_element_type=F32)


def iota(shape, dim):
    return lax.broadcasted_iota(jnp.int32, shape, dim)


def halves(v):
    hi = v.astype(BF16)
    return hi, (v - hi.astype(F32)).astype(BF16)


def kernel(
    tok_ref, cot_ref, ids_ref, gates_ref, gw_ref, uw_ref, dw_ref,
    mixed_ref, igrad_ref, gg_ref, ggw_ref, guw_ref,
    W, AGT, AGC, STG, ROW, PCOT, XS, XT, HG, HU, ACT, DGU, OST, RET, PARTM, PARTX, RSSM, RSSX, RSRM, RSRX, ONE, TG, EX, WG, TO,
    w_s, w_r, l_s, ag_s, ag_r, di_s, di_r, re_s, re_r, rs_s, rs_r, xs_s, xs_r, dg_s, dg_r,
):
    x = lax.axis_index("dp")
    e = lax.axis_index("expert")
    z = e // NJ
    j = lax.rem(e, NJ)

    def zpeer(d):
        return {"dp": x, "expert": lax.rem(z + d + NZ, NZ) * NJ + j}

    def jat(q):
        return lax.rem(j + q + NJ, NJ)

    def xat(q):
        return lax.rem(x + q + NX, NX)

    def jpeer(q):
        return {"dp": x, "expert": z * NJ + jat(q)}

    def xpeer(q):
        return {"dp": xat(q), "expert": e}

    def local(src, dst, sem):
        copy = pltpu.make_async_copy(src, dst, sem)
        copy.start()
        return copy

    first = [local(tok_ref, AGT.at[4, :, pl.ds(0, D)], l_s.at[3]), local(cot_ref, AGC.at[4], l_s.at[4])]
    own = [local(ref.at[0], W.at[i, x], l_s.at[i]) for i, ref in enumerate((gw_ref, uw_ref, dw_ref))]

    barrier = pltpu.get_barrier_semaphore()
    peers = [zpeer(d) for d in (1, -1)] + [jpeer(q) for q in range(1, NJ)] + [xpeer(q) for q in range(1, NX)]
    for peer in peers:
        pl.semaphore_signal(barrier, inc=1, device_id=peer, device_id_type=MESH)

    spread = (lax.rem(iota((TOK, 128), 1), TOK) == iota((TOK, 128), 0)).astype(F32)
    here = iota((TOP, 128), 1) // TOK == iota((TOP, 128), 0)

    def flat(v):
        return jnp.sum(jnp.where(here, dot(v, spread), 0.0), axis=0, keepdims=True)

    ids = flat(ids_ref[...].astype(F32))
    hi, lo = halves(gates_ref[...])
    table = jnp.broadcast_to(ids, (128, 128))
    again = (table == table.T) & (iota((128, 128), 0) < iota((128, 128), 1))
    code = ids * 2.0 + jnp.sum(again.astype(F32), axis=0, keepdims=True)
    row = iota((TOK, 128), 0)
    meta = jnp.where(row == 0, code, jnp.where(row == 1, flat(hi.astype(F32)), jnp.where(row == 2, flat(lo.astype(F32)), 0.0)))
    AGT[4, :, D:] = meta.astype(BF16)
    pl.semaphore_wait(barrier, len(peers))

    sent = []

    def send(src, dst, s, r, peer):
        copy = pltpu.make_async_remote_copy(
            src_ref=src, dst_ref=dst, send_sem=s, recv_sem=r, device_id=peer, device_id_type=MESH
        )
        copy.start()
        sent.append(copy)
        return copy

    AG = (AGT, AGC)
    arrive = {}

    CUT = D // 2
    PIECES = ((pl.ds(0, CUT), pl.ds(CUT, WIDE - CUT)), (pl.ds(0, CUT), pl.ds(CUT, D - CUT)))

    def ag_send(tc, half, r, step):
        to = (r - step) % NZ
        at = PIECES[tc][half]
        arrive[tc, half, to] = send(
            AG[tc].at[r, :, at], AG[tc].at[to, :, at], ag_s.at[tc, half, to], ag_r.at[tc, half, to], zpeer(step)
        )

    def ring(h):
        for tc in (0, 1):
            if h == 0:
                first[tc].wait()
            for half in (0, 1):
                if h > 0:
                    arrive[tc, half, (4 - h) % NZ].wait_recv()
                if h < 8:
                    ag_send(tc, half, (4 - h) % NZ, 1)
                if 0 < h < 8:
                    arrive[tc, half, 4 + h].wait_recv()
                if h < 7:
                    ag_send(tc, half, 4 + h, -1)

    HALF = COLS // 2
    weights = {}
    relays = {}

    def weight_out(i):
        ref = (gw_ref, uw_ref, dw_ref)[i]
        for q in (1, 3):
            weights[i, q] = send(ref.at[0], W.at[i, x], w_s.at[i, q], w_r.at[i, q], xpeer(q))

    def relay(i):
        for q, half in ((1, 0), (3, 1)):
            weights[i, q].wait_recv()
            block = W.at[i, xat(-q), pl.ds(half * HALF, HALF)]
            relays[i, half] = send(block, block, w_s.at[i, 2 * half], w_r.at[i, 2 * half], xpeer(q))

    def select(ch):
        m = AGT[pl.ds(NB * ch, NB), :, D:].reshape(ROWS, 128)
        row, col = iota((ROWS, ROWS), 0), iota((ROWS, ROWS), 1)
        mine = lax.rem(row, 16) // 2 * TOK
        codes = dot((col == mine).astype(F32).astype(BF16), m)
        gates = dot(((col == mine + 1) | (col == mine + 2)).astype(F32).astype(BF16), m)
        row = iota((ROWS, 128), 0)
        col = iota((ROWS, 128), 1)
        want = ((z * NJ + row // 16) * 2 + lax.rem(row, 2)).astype(F32)
        taken = (codes == want).astype(F32)
        gate = jnp.sum(taken * gates, axis=1, keepdims=True)
        fold = (lax.rem(row, TOK) == lax.rem(col, TOK)).astype(F32).astype(BF16)
        one = dot(taken.astype(BF16), fold)
        one = jnp.where(lax.rem(row, 16) // 2 == col // TOK, one, 0.0)
        EX[ch] = taken.astype(BF16)
        ONE[ch] = one.astype(BF16)
        one_t = one.T
        TG[ch, 0] = one_t.astype(BF16)
        gated = (one * gate).T
        hi, lo = halves(gated)
        TG[ch, 1] = hi
        TG[ch, 2] = lo
        return gate

    rows_in = {}

    def pack(tc, ch, gate):
        one = ONE[ch]

        @pl.loop(0, D // COLS)
        def _(n):
            at = pl.ds(pl.multiple_of(n * COLS, COLS), COLS)
            picked = dot(one, AG[tc][pl.ds(NB * ch, NB), :, at].reshape(ROWS, COLS))
            if tc == 1:
                PCOT[ch, :, at] = picked.astype(BF16)
                picked = picked * gate
            STG[ch, tc, :, :, at] = picked.astype(BF16).reshape(NJ, 16, COLS)

        for q in range(1, NJ):
            rows_in[ch, tc, q] = send(
                STG.at[ch, tc, jat(q)], ROW.at[tc, ch, j], di_s.at[ch, tc, q], di_r.at[ch, tc, q], jpeer(q)
            )
        ROW[tc, ch, j] = STG[ch, tc, j]

    def rows_wait(tc):
        for ch in (0, 1):
            for q in range(1, NJ):
                rows_in[ch, tc, q].wait_recv()

    ring(0)
    weight_out(0)
    weight_out(1)
    ring(1)
    ring(2)
    ring(3)
    weight_out(2)
    ring(4)
    gate_a = select(0)
    pack(0, 0, gate_a)
    ring(5)
    pack(1, 0, gate_a)
    relay(0)
    relay(1)
    ring(6)
    ring(7)
    relay(2)
    ring(8)
    gate_b = select(1)
    pack(0, 1, gate_b)
    pack(1, 1, gate_b)
    rows_wait(0)

    slices = []
    for q in (2, 1, 3):
        at = pl.ds(pl.multiple_of(xat(q) * COLS, COLS), COLS)
        slices.append(send(ROW.at[0, :, :, :, at], XS.at[x], xs_s.at[q], xs_r.at[q], xpeer(q)))
    XS[x] = ROW[0, :, :, :, pl.ds(pl.multiple_of(x * COLS, COLS), COLS)]

    def weight_in(i):
        own[i].wait()
        for half in (0, 1):
            relays[i, half].wait_recv()

    def rows_by(i, tc, to):
        to[...] = jnp.zeros_like(to)

        @pl.loop(0, NX)
        def _(n):
            at = pl.ds(pl.multiple_of(n * COLS, COLS), COLS)
            to[...] += dot(ROW[tc, :, :, :, at].reshape(2 * ROWS, COLS), W[i, n])

    weight_in(0)
    rows_by(0, 0, HG)
    weight_in(1)
    rows_by(1, 0, HU)
    hg, hu = HG[...], HU[...]
    sigma = jax.nn.sigmoid(hg)
    ACT[...] = (hg * sigma * hu).astype(BF16)
    weight_in(2)

    back = {}

    def give_back(arr, ch):
        for q in range(1, NJ):
            back[arr, ch, q] = send(
                OST.at[arr, ch, jat(q)], RET.at[arr, ch, j], re_s.at[arr, ch, q], re_r.at[arr, ch, q], jpeer(q)
            )
        RET[arr, ch, j] = OST[arr, ch, j]

    @pl.loop(0, NX)
    def _(n):
        at = pl.ds(pl.multiple_of(n * COLS, COLS), COLS)
        OST[0, :, :, :, at] = dot_t(ACT[...], W[2, n]).astype(BF16).reshape(2, NJ, 16, COLS)

    PART, RSS, RSR = (PARTM, PARTX), (RSSM, RSSX), (RSRM, RSRX)

    def combine(arr, ch):
        for q in range(1, NJ):
            back[arr, ch, q].wait_recv()

        def step(n, dots):
            at = pl.ds(pl.multiple_of(n * COLS, COLS), COLS)
            block = RET[arr, ch, :, :, at].reshape(ROWS, COLS)
            if arr == 0:
                part = dot(TG[ch, 1], block) + dot(TG[ch, 2], block)
                dots = dots + jnp.sum(block.astype(F32) * PCOT[ch, :, at].astype(F32), axis=1, keepdims=True)
            else:
                part = dot(TG[ch, 0], block)
            PART[arr][pl.ds(NB * ch, NB), :, at] = part.reshape(NB, TOK, COLS)
            return dots

        dots = lax.fori_loop(0, D // COLS, step, jnp.zeros((ROWS, 1), F32))
        if arr == 0:
            hi, lo = halves(EX[ch].astype(F32) * dots)
            row, col = iota((ROWS, ROWS), 0), iota((ROWS, ROWS), 1)
            first = lax.rem(col, 16) // 2 * TOK
            grads = dot((row == first).astype(F32).astype(BF16), hi) + dot((row == first + 1).astype(F32).astype(BF16), lo)
            PARTM[pl.ds(NB * ch, NB), :, D:] = grads.reshape(NB, TOK, 128)

    arrived = {}

    def rs_sum(arr, half, r, *others):
        at = PIECES[arr][half]
        value = PART[arr][r, :, at]
        for other in others:
            arrived[arr, half, other].wait_recv()
            value = value + RSR[arr][other, :, at].astype(F32)
        return value

    def rs_send(arr, r, step, *others):
        for half in (0, 1):
            at = PIECES[arr][half]
            RSS[arr][r, :, at] = rs_sum(arr, half, r, *others).astype(BF16)
            arrived[arr, half, r] = send(
                RSS[arr].at[r, :, at], RSR[arr].at[r, :, at], rs_s.at[arr, half, r], rs_r.at[arr, half, r], zpeer(step)
            )

    def hop(arr, h):
        r = (12 + h) % NZ
        rs_send(arr, r, -1, *(((r - 1) % NZ,) if h else ()))
        if h < 7:
            rs_send(arr, 11 - h, 1, *((12 - h,) if h else ()))

    give_back(0, 1)
    rows_wait(1)
    rows_by(2, 1, HU)
    da = HU[...]
    DGU[x, 1] = (da * hg * sigma).astype(BF16)
    DGU[x, 0] = (da * hu * sigma * (1.0 + hg * (1.0 - sigma))).astype(BF16)
    grads = [send(DGU.at[x], DGU.at[x], dg_s.at[q], dg_r.at[q], xpeer(q)) for q in (2, 1, 3)]

    @pl.loop(0, NX)
    def _(n):
        at = pl.ds(pl.multiple_of(n * COLS, COLS), COLS)
        dx = dot_t(DGU[x, 0], W[0, n]) + dot_t(DGU[x, 1], W[1, n])
        OST[1, :, :, :, at] = dx.astype(BF16).reshape(2, NJ, 16, COLS)

    give_back(1, 1)
    give_back(0, 0)
    give_back(1, 0)
    combine(0, 1)
    hop(0, 0)
    combine(1, 1)
    hop(1, 0)
    hop(0, 1)
    for copy in slices:
        copy.wait_recv()

    @pl.loop(0, NX)
    def _(n):
        XT[n] = XS[n].reshape(2 * ROWS, COLS).T

    hop(1, 1)
    hop(0, 2)
    hop(1, 2)
    hop(0, 3)
    combine(0, 0)
    hop(1, 3)
    hop(0, 4)
    combine(1, 0)
    for h in (4, 5, 6):
        hop(1, h)
        hop(0, h + 1)
    hop(1, 7)
    for copy in grads:
        copy.wait_recv()
    WG[...] = jnp.zeros_like(WG)

    @pl.loop(0, NX)
    def _(n):
        WG[0] += dot(XT[n], DGU[n, 0])
        WG[1] += dot(XT[n], DGU[n, 1])

    out = [local(WG.at[0], ggw_ref.at[0], l_s.at[5]), local(WG.at[1], guw_ref.at[0], l_s.at[6])]
    TO[0, :, :CUT] = rs_sum(0, 0, 4, 3, 5).astype(BF16)
    total = rs_sum(0, 1, 4, 3, 5)
    TO[0, :, CUT:] = total[:, : D - CUT].astype(BF16)
    total = total[:, D - CUT :]
    out.append(local(TO.at[0], mixed_ref, l_s.at[7]))
    mine = jnp.where(iota((TOK, 128), 1) // TOK == row, total[0:1] + total[1:2], 0.0)
    hi, lo = halves(mine)
    unfold = (lax.rem(iota((128, TOK), 0), TOK) == iota((128, TOK), 1)).astype(F32).astype(BF16)
    gg_ref[...] = (dot(hi, unfold) + dot(lo, unfold))[:TOP]
    TO[1, :, :CUT] = rs_sum(1, 0, 4, 3, 5).astype(BF16)
    TO[1, :, CUT:] = rs_sum(1, 1, 4, 3, 5).astype(BF16)
    out.append(local(TO.at[1], igrad_ref, l_s.at[8]))
    for copy in sent:
        copy.wait_send()
    for copy in out:
        copy.wait()


def body(tokens, cotangent, expert_ids, gate_values, gate_weight, up_weight, down_weight):
    vmem = pl.BlockSpec(memory_space=pltpu.VMEM)
    hbm = pl.BlockSpec(memory_space=pltpu.HBM)
    dma = pltpu.SemaphoreType.DMA
    v = pltpu.VMEM
    outs = (
        jax.ShapeDtypeStruct((TOK, D), BF16),
        jax.ShapeDtypeStruct((TOK, D), BF16),
        jax.ShapeDtypeStruct((TOP, TOK), F32),
        jax.ShapeDtypeStruct((1, COLS, H), F32),
        jax.ShapeDtypeStruct((1, COLS, H), F32),
    )
    mixed, igrad, gg, ggw, guw = pl.pallas_call(
        kernel,
        out_shape=outs,
        in_specs=[hbm] * 2 + [vmem] * 2 + [hbm] * 3,
        out_specs=[hbm] * 2 + [vmem] + [hbm] * 2,
        scratch_shapes=[
            v((3, NX, COLS, H), BF16),
            v((NZ, TOK, WIDE), BF16),
            v((NZ, TOK, D), BF16),
            v((2, 2, NJ, 16, D), BF16),
            v((2, 2, NJ, 16, D), BF16),
            v((2, ROWS, D), BF16),
            v((NX, 2, NJ, 16, COLS), BF16),
            v((NX, COLS, 2 * ROWS), BF16),
            v((2 * ROWS, H), F32),
            v((2 * ROWS, H), F32),
            v((2 * ROWS, H), BF16),
            v((NX, 2, 2 * ROWS, H), BF16),
            v((2, 2, NJ, 16, D), BF16),
            v((2, 2, NJ, 16, D), BF16),
            v((NZ, TOK, WIDE), F32),
            v((NZ, TOK, D), F32),
            v((NZ, TOK, WIDE), BF16),
            v((NZ, TOK, D), BF16),
            v((NZ, TOK, WIDE), BF16),
            v((NZ, TOK, D), BF16),
            v((2, ROWS, ROWS), BF16),
            v((2, 3, ROWS, ROWS), BF16),
            v((2, ROWS, 128), BF16),
            v((2, COLS, H), F32),
            v((2, TOK, D), BF16),
            dma((3, NX)), dma((3, NX)), dma((9,)),
            dma((2, 2, NZ)), dma((2, 2, NZ)),
            dma((2, 2, NJ)), dma((2, 2, NJ)),
            dma((2, 2, NJ)), dma((2, 2, NJ)),
            dma((2, 2, NZ)), dma((2, 2, NZ)),
            dma((NX,)), dma((NX,)),
            dma((NX,)), dma((NX,)),
        ],
        compiler_params=pltpu.CompilerParams(
            collective_id=0, has_side_effects=True, vmem_limit_bytes=60 * 2**20
        ),
        name="experts",
    )(tokens, cotangent, expert_ids.T, gate_values.T, gate_weight, up_weight, down_weight)
    return mixed, igrad, gg.T, ggw, guw


def solution(mesh):
    token = P(("dp", "expert"), None)
    weight = P("expert", "dp", None)
    return jax.shard_map(
        body,
        mesh=mesh,
        in_specs=(token,) * 4 + (weight,) * 3,
        out_specs=(token,) * 3 + (weight,) * 2,
        check_vma=False,
    )
```

```python
import functools

import jax
import jax.numpy as jnp
from jax import lax
from jax.experimental import pallas as pl
from jax.experimental.pallas import tpu as pltpu
from jax.sharding import PartitionSpec as P

MESH = pl.DeviceIdType.MESH
NX, NZ, NJ = 4, 16, 8
TOK, D, H, TOP = 16, 2048, 384, 8
NB = 8
ROWS = NB * TOK
COLS = 512
SPLIT = 2
WIDE = D + 128
F32, BF16 = jnp.float32, jnp.bfloat16
NT = (((1,), (1,)), ((), ()))


def dot(a, b):
    return jnp.dot(a, b, preferred_element_type=F32)


def dot_t(a, b):
    return lax.dot_general(a, b, NT, preferred_element_type=F32)


def iota(shape, dim):
    return lax.broadcasted_iota(jnp.int32, shape, dim)


def halves(v):
    hi = v.astype(BF16)
    return hi, (v - hi.astype(F32)).astype(BF16)


def kernel(
    tok_ref, cot_ref, ids_ref, gates_ref, gw_ref, uw_ref, dw_ref,
    token_out, gg_ref, weight_out_ref,
    W, AGT, AGC, STG, ROW, PCOT, XS, XT, HG, HU, ACT, DGU, OST, RET, PARTM, PARTX, RSSM, RSSX, RSRM, RSRX, ONE, TG, EX, WG, TO,
    w_s, w_r, l_s, ag_s, ag_r, di_s, di_r, re_s, re_r, rs_s, rs_r, xs_s, xs_r, dg_s, dg_r,
):
    x = lax.axis_index("dp")
    e = lax.axis_index("expert")
    z = e // NJ
    j = lax.rem(e, NJ)

    def zpeer(d):
        return {"dp": x, "expert": lax.rem(z + d + NZ, NZ) * NJ + j}

    def jat(q):
        return lax.rem(j + q + NJ, NJ)

    def xat(q):
        return lax.rem(x + q + NX, NX)

    def jpeer(q):
        return {"dp": x, "expert": z * NJ + jat(q)}

    def xpeer(q):
        return {"dp": xat(q), "expert": e}

    def local(src, dst, sem):
        copy = pltpu.make_async_copy(src, dst, sem)
        copy.start()
        return copy

    first = [local(tok_ref, AGT.at[4, :, pl.ds(0, D)], l_s.at[3]), local(cot_ref, AGC.at[4], l_s.at[4])]
    own = [local(ref.at[0], W.at[i, x], l_s.at[i]) for i, ref in enumerate((gw_ref, uw_ref, dw_ref))]

    barrier = pltpu.get_barrier_semaphore()
    peers = [zpeer(d) for d in (1, -1)] + [jpeer(q) for q in range(1, NJ)] + [xpeer(q) for q in range(1, NX)]
    for peer in peers:
        pl.semaphore_signal(barrier, inc=1, device_id=peer, device_id_type=MESH)

    spread = (lax.rem(iota((TOK, 128), 1), TOK) == iota((TOK, 128), 0)).astype(F32)
    here = iota((TOP, 128), 1) // TOK == iota((TOP, 128), 0)

    def flat(v):
        return jnp.sum(jnp.where(here, dot(v, spread), 0.0), axis=0, keepdims=True)

    ids = flat(ids_ref[...].astype(F32))
    hi, lo = halves(gates_ref[...])
    table = jnp.broadcast_to(ids, (128, 128))
    again = (table == table.T) & (iota((128, 128), 0) < iota((128, 128), 1))
    code = ids * 2.0 + jnp.sum(again.astype(F32), axis=0, keepdims=True)
    row = iota((TOK, 128), 0)
    meta = jnp.where(row == 0, code, jnp.where(row == 1, flat(hi.astype(F32)), jnp.where(row == 2, flat(lo.astype(F32)), 0.0)))
    AGT[4, :, D:] = meta.astype(BF16)
    pl.semaphore_wait(barrier, len(peers))

    sent = []

    def send(src, dst, s, r, peer):
        copy = pltpu.make_async_remote_copy(
            src_ref=src, dst_ref=dst, send_sem=s, recv_sem=r, device_id=peer, device_id_type=MESH
        )
        copy.start()
        sent.append(copy)
        return copy

    AG = (AGT, AGC)
    arrive = {}

    CUT = D // SPLIT
    LAST = D - CUT
    PIECES = [[pl.ds(i * CUT, CUT) for i in range(SPLIT - 1)] + [pl.ds(LAST, end - LAST)] for end in (WIDE, D)]

    def ag_send(tc, half, r, step):
        to = (r - step) % NZ
        at = PIECES[tc][half]
        arrive[tc, half, to] = send(
            AG[tc].at[r, :, at], AG[tc].at[to, :, at], ag_s.at[tc, half, to], ag_r.at[tc, half, to], zpeer(step)
        )

    def ring(h):
        for tc in (0, 1):
            if h == 0:
                first[tc].wait()
            for half in range(SPLIT):
                if h > 0:
                    arrive[tc, half, (4 - h) % NZ].wait_recv()
                if h < 8:
                    ag_send(tc, half, (4 - h) % NZ, 1)
                if 0 < h < 8:
                    arrive[tc, half, 4 + h].wait_recv()
                if h < 7:
                    ag_send(tc, half, 4 + h, -1)

    HALF = COLS // 2
    weights = {}
    relays = {}

    def weight_out(i):
        ref = (gw_ref, uw_ref, dw_ref)[i]
        for q in (1, 3):
            weights[i, q] = send(ref.at[0], W.at[i, x], w_s.at[i, q], w_r.at[i, q], xpeer(q))

    def relay(i):
        for q, half in ((1, 0), (3, 1)):
            weights[i, q].wait_recv()
            block = W.at[i, xat(-q), pl.ds(half * HALF, HALF)]
            relays[i, half] = send(block, block, w_s.at[i, 2 * half], w_r.at[i, 2 * half], xpeer(q))

    def select(ch):
        m = AGT[pl.ds(NB * ch, NB), :, D:].reshape(ROWS, 128)
        row, col = iota((ROWS, ROWS), 0), iota((ROWS, ROWS), 1)
        mine = lax.rem(row, 16) // 2 * TOK
        codes = dot((col == mine).astype(F32).astype(BF16), m)
        gates = dot(((col == mine + 1) | (col == mine + 2)).astype(F32).astype(BF16), m)
        row = iota((ROWS, 128), 0)
        col = iota((ROWS, 128), 1)
        want = ((z * NJ + row // 16) * 2 + lax.rem(row, 2)).astype(F32)
        taken = (codes == want).astype(F32)
        gate = jnp.sum(taken * gates, axis=1, keepdims=True)
        fold = (lax.rem(row, TOK) == lax.rem(col, TOK)).astype(F32).astype(BF16)
        one = dot(taken.astype(BF16), fold)
        one = jnp.where(lax.rem(row, 16) // 2 == col // TOK, one, 0.0)
        EX[ch] = taken.astype(BF16)
        ONE[ch] = one.astype(BF16)
        one_t = one.T
        TG[ch, 0] = one_t.astype(BF16)
        gated = (one * gate).T
        hi, lo = halves(gated)
        TG[ch, 1] = hi
        TG[ch, 2] = lo
        return gate

    rows_in = {}

    def pack(tc, ch, gate):
        one = ONE[ch]

        @pl.loop(0, D // COLS)
        def _(n):
            at = pl.ds(pl.multiple_of(n * COLS, COLS), COLS)
            picked = dot(one, AG[tc][pl.ds(NB * ch, NB), :, at].reshape(ROWS, COLS))
            if tc == 1:
                PCOT[ch, :, at] = picked.astype(BF16)
                picked = picked * gate
            STG[ch, tc, :, :, at] = picked.astype(BF16).reshape(NJ, 16, COLS)

        for q in range(1, NJ):
            rows_in[ch, tc, q] = send(
                STG.at[ch, tc, jat(q)], ROW.at[tc, ch, j], di_s.at[ch, tc, q], di_r.at[ch, tc, q], jpeer(q)
            )
        ROW[tc, ch, j] = STG[ch, tc, j]

    def rows_wait(tc):
        for ch in (0, 1):
            for q in range(1, NJ):
                rows_in[ch, tc, q].wait_recv()

    ring(0)
    weight_out(0)
    weight_out(1)
    ring(1)
    ring(2)
    ring(3)
    weight_out(2)
    ring(4)
    gate_a = select(0)
    pack(0, 0, gate_a)
    ring(5)
    pack(1, 0, gate_a)
    relay(0)
    relay(1)
    ring(6)
    ring(7)
    relay(2)
    ring(8)
    gate_b = select(1)
    pack(0, 1, gate_b)
    pack(1, 1, gate_b)
    rows_wait(0)

    slices = []
    for q in (2, 1, 3):
        at = pl.ds(pl.multiple_of(xat(q) * COLS, COLS), COLS)
        slices.append(send(ROW.at[0, :, :, :, at], XS.at[x], xs_s.at[q], xs_r.at[q], xpeer(q)))
    XS[x] = ROW[0, :, :, :, pl.ds(pl.multiple_of(x * COLS, COLS), COLS)]

    def weight_in(i):
        own[i].wait()
        for half in (0, 1):
            relays[i, half].wait_recv()

    def rows_by(i, tc, to):
        to[...] = jnp.zeros_like(to)

        @pl.loop(0, NX)
        def _(n):
            at = pl.ds(pl.multiple_of(n * COLS, COLS), COLS)
            to[...] += dot(ROW[tc, :, :, :, at].reshape(2 * ROWS, COLS), W[i, n])

    weight_in(0)
    rows_by(0, 0, HG)
    weight_in(1)
    rows_by(1, 0, HU)
    hg, hu = HG[...], HU[...]
    sigma = jax.nn.sigmoid(hg)
    ACT[...] = (hg * sigma * hu).astype(BF16)
    weight_in(2)

    back = {}

    def give_back(arr, ch):
        for q in range(1, NJ):
            back[arr, ch, q] = send(
                OST.at[arr, ch, jat(q)], RET.at[arr, ch, j], re_s.at[arr, ch, q], re_r.at[arr, ch, q], jpeer(q)
            )
        RET[arr, ch, j] = OST[arr, ch, j]

    PART, RSS, RSR = (PARTM, PARTX), (RSSM, RSSX), (RSRM, RSRX)

    def combine(arr, ch):
        for q in range(1, NJ):
            back[arr, ch, q].wait_recv()

        def step(n, dots):
            at = pl.ds(pl.multiple_of(n * COLS, COLS), COLS)
            block = RET[arr, ch, :, :, at].reshape(ROWS, COLS)
            if arr == 0:
                part = dot(TG[ch, 1], block) + dot(TG[ch, 2], block)
                dots = dots + jnp.sum(block.astype(F32) * PCOT[ch, :, at].astype(F32), axis=1, keepdims=True)
            else:
                part = dot(TG[ch, 0], block)
            PART[arr][pl.ds(NB * ch, NB), :, at] = part.reshape(NB, TOK, COLS)
            return dots

        dots = lax.fori_loop(0, D // COLS, step, jnp.zeros((ROWS, 1), F32))
        if arr == 0:
            hi, lo = halves(EX[ch].astype(F32) * dots)
            row, col = iota((ROWS, ROWS), 0), iota((ROWS, ROWS), 1)
            first = lax.rem(col, 16) // 2 * TOK
            grads = dot((row == first).astype(F32).astype(BF16), hi) + dot((row == first + 1).astype(F32).astype(BF16), lo)
            PARTM[pl.ds(NB * ch, NB), :, D:] = grads.reshape(NB, TOK, 128)

    arrived = {}

    def rs_sum(arr, half, r, *others):
        at = PIECES[arr][half]
        value = PART[arr][r, :, at]
        for other in others:
            arrived[arr, half, other].wait_recv()
            value = value + RSR[arr][other, :, at].astype(F32)
        return value

    def rs_send(arr, r, step, *others):
        for half in range(SPLIT):
            at = PIECES[arr][half]
            RSS[arr][r, :, at] = rs_sum(arr, half, r, *others).astype(BF16)
            arrived[arr, half, r] = send(
                RSS[arr].at[r, :, at], RSR[arr].at[r, :, at], rs_s.at[arr, half, r], rs_r.at[arr, half, r], zpeer(step)
            )

    def hop(arr, h):
        r = (12 + h) % NZ
        rs_send(arr, r, -1, *(((r - 1) % NZ,) if h else ()))
        if h < 7:
            rs_send(arr, 11 - h, 1, *((12 - h,) if h else ()))

    def outputs(ch):
        half = slice(ch * ROWS, ch * ROWS + ROWS)

        @pl.loop(0, NX)
        def _(n):
            at = pl.ds(pl.multiple_of(n * COLS, COLS), COLS)
            OST[0, ch, :, :, at] = dot_t(ACT[half], W[2, n]).astype(BF16).reshape(NJ, 16, COLS)

    def input_grads(ch):
        half = slice(ch * ROWS, ch * ROWS + ROWS)

        @pl.loop(0, NX)
        def _(n):
            at = pl.ds(pl.multiple_of(n * COLS, COLS), COLS)
            dx = dot_t(DGU[x, 0, half], W[0, n]) + dot_t(DGU[x, 1, half], W[1, n])
            OST[1, ch, :, :, at] = dx.astype(BF16).reshape(NJ, 16, COLS)

    outputs(1)
    give_back(0, 1)
    rows_wait(1)
    rows_by(2, 1, HU)
    da = HU[...]
    DGU[x, 1] = (da * hg * sigma).astype(BF16)
    DGU[x, 0] = (da * hu * sigma * (1.0 + hg * (1.0 - sigma))).astype(BF16)
    grads = [send(DGU.at[x], DGU.at[x], dg_s.at[q], dg_r.at[q], xpeer(q)) for q in (2, 1, 3)]

    input_grads(1)
    give_back(1, 1)
    outputs(0)
    give_back(0, 0)
    input_grads(0)
    give_back(1, 0)
    combine(0, 1)
    hop(0, 0)
    combine(1, 1)
    hop(1, 0)
    hop(0, 1)
    for copy in slices:
        copy.wait_recv()

    @pl.loop(0, NX)
    def _(n):
        XT[n] = XS[n].reshape(2 * ROWS, COLS).T

    hop(1, 1)
    hop(0, 2)
    hop(1, 2)
    hop(0, 3)
    combine(0, 0)
    hop(1, 3)
    hop(0, 4)
    combine(1, 0)
    for h in (4, 5, 6):
        hop(1, h)
        hop(0, h + 1)
    hop(1, 7)
    for copy in grads:
        copy.wait_recv()
    WG[...] = jnp.zeros_like(WG)

    @pl.loop(0, NX)
    def _(n):
        WG[0] += dot(XT[n], DGU[n, 0])
        WG[1] += dot(XT[n], DGU[n, 1])

    out = [local(WG, weight_out_ref, l_s.at[5])]
    for i in range(SPLIT - 1):
        TO[0, :, PIECES[0][i]] = rs_sum(0, i, 4, 3, 5).astype(BF16)
    total = rs_sum(0, SPLIT - 1, 4, 3, 5)
    TO[0, :, LAST:] = total[:, :CUT].astype(BF16)
    total = total[:, CUT:]
    out.append(local(TO.at[0], token_out.at[0], l_s.at[6]))
    mine = jnp.where(iota((TOK, 128), 1) // TOK == row, total[0:1] + total[1:2], 0.0)
    hi, lo = halves(mine)
    unfold = (lax.rem(iota((128, TOK), 0), TOK) == iota((128, TOK), 1)).astype(F32).astype(BF16)
    gg_ref[...] = (dot(hi, unfold) + dot(lo, unfold))[:TOP]
    for i in range(SPLIT):
        TO[1, :, PIECES[1][i]] = rs_sum(1, i, 4, 3, 5).astype(BF16)
    out.append(local(TO.at[1], token_out.at[1], l_s.at[7]))
    for copy in sent:
        copy.wait_send()
    for copy in out:
        copy.wait()


def body(tokens, cotangent, expert_ids, gate_values, gate_weight, up_weight, down_weight):
    vmem = pl.BlockSpec(memory_space=pltpu.VMEM)
    hbm = pl.BlockSpec(memory_space=pltpu.HBM)
    dma = pltpu.SemaphoreType.DMA
    v = pltpu.VMEM
    outs = (
        jax.ShapeDtypeStruct((2, TOK, D), BF16),
        jax.ShapeDtypeStruct((TOP, TOK), F32),
        jax.ShapeDtypeStruct((2, COLS, H), F32),
    )
    token_grads, gg, weight_grads = pl.pallas_call(
        kernel,
        out_shape=outs,
        in_specs=[hbm] * 2 + [vmem] * 2 + [hbm] * 3,
        out_specs=[hbm, vmem, hbm],
        scratch_shapes=[
            v((3, NX, COLS, H), BF16),
            v((NZ, TOK, WIDE), BF16),
            v((NZ, TOK, D), BF16),
            v((2, 2, NJ, 16, D), BF16),
            v((2, 2, NJ, 16, D), BF16),
            v((2, ROWS, D), BF16),
            v((NX, 2, NJ, 16, COLS), BF16),
            v((NX, COLS, 2 * ROWS), BF16),
            v((2 * ROWS, H), F32),
            v((2 * ROWS, H), F32),
            v((2 * ROWS, H), BF16),
            v((NX, 2, 2 * ROWS, H), BF16),
            v((2, 2, NJ, 16, D), BF16),
            v((2, 2, NJ, 16, D), BF16),
            v((NZ, TOK, WIDE), F32),
            v((NZ, TOK, D), F32),
            v((NZ, TOK, WIDE), BF16),
            v((NZ, TOK, D), BF16),
            v((NZ, TOK, WIDE), BF16),
            v((NZ, TOK, D), BF16),
            v((2, ROWS, ROWS), BF16),
            v((2, 3, ROWS, ROWS), BF16),
            v((2, ROWS, 128), BF16),
            v((2, COLS, H), F32),
            v((2, TOK, D), BF16),
            dma((3, NX)), dma((3, NX)), dma((8,)),
            dma((2, SPLIT, NZ)), dma((2, SPLIT, NZ)),
            dma((2, 2, NJ)), dma((2, 2, NJ)),
            dma((2, 2, NJ)), dma((2, 2, NJ)),
            dma((2, SPLIT, NZ)), dma((2, SPLIT, NZ)),
            dma((NX,)), dma((NX,)),
            dma((NX,)), dma((NX,)),
        ],
        compiler_params=pltpu.CompilerParams(
            collective_id=0, has_side_effects=True, vmem_limit_bytes=60 * 2**20
        ),
        name="experts",
    )(tokens, cotangent, expert_ids.T, gate_values.T, gate_weight, up_weight, down_weight)
    return token_grads[0], token_grads[1], gg.T, weight_grads[:1], weight_grads[1:]


def solution(mesh):
    token = P(("dp", "expert"), None)
    weight = P("expert", "dp", None)
    return jax.shard_map(
        body,
        mesh=mesh,
        in_specs=(token,) * 4 + (weight,) * 3,
        out_specs=(token,) * 3 + (weight,) * 2,
        check_vma=False,
    )
```
